32 devices in a mesh: req: 8 (over z, x), head: 4 (over y, core).
Axes of the slice: x: 2, y: 2, z: 4, core: 2. Of those that a mesh axis runs over, the one named last changes fastest.
Arguments:
- residual: bfloat16 [128, 4096], P(None, 'req'), may hold values from -80 to 80
- lengths: int32 [128], P('req'), may hold values from 0 to 32768, as said below
- ssm_state: float32 [128, 128, 64, 128], P('req', 'head'), may hold values from -6 to 6
- tail_mix: float32 [128, 3, 8192], P('req', None, 'head'), may hold values from -6 to 6
- tail_group: float32 [128, 3, 2, 1024], P('req', None, None, 'head'), may hold values from -6 to 6
- norm_first: float32 [4096], P('req'), may hold values from 0.1 to 1.9
- mix_weight: bfloat16 [4096, 2, 8192], P('req', None, 'head'), may hold values from -0.09375 to 0.09375
- group_weight: bfloat16 [4096, 2, 1024], P('req', None, 'head'), may hold values from -0.09375 to 0.09375
- step_weight: bfloat16 [4096, 128], P('req', 'head'), may hold values from -0.09375 to 0.09375
- conv_mix: float32 [4, 8192], P(None, 'head'), may hold values from -3 to 3
- conv_group: float32 [4, 2, 1024], P(None, None, 'head'), may hold values from -3 to 3
- bias_mix: float32 [8192], P('head'), may hold values from -3 to 3
- bias_group: float32 [2, 1024], P(None, 'head'), may hold values from -3 to 3
- step_bias: float32 [128], P('head'), may hold values from -2 to 1
- decay_log: float32 [128], P('head'), may hold values from -1 to 2
- skip_gain: float32 [128], P('head'), may hold values from 0.5 to 2
- gate_gain: float32 [8192], P('head'), may hold values from 0.1 to 1.9
- out_weight: bfloat16 [8192, 4096], P('head', 'req'), may hold values from -0.0625 to 0.0625
- norm_second: float32 [4096], P('req'), may hold values from 0.1 to 1.9
- up_weight: bfloat16 [4096, 21504], P('req', 'head'), may hold values from -0.09375 to 0.09375
- down_weight: bfloat16 [21504, 4096], P('head', 'req'), may hold values from -0.0390625 to 0.0390625
Outputs:
- residual_out: bfloat16 [128, 4096], P(None, 'req')
- state_out: float32 [128, 128, 64, 128], P('req', 'head')
- tail_mix_out: float32 [128, 3, 8192], P('req', None, 'head')
- tail_group_out: float32 [128, 3, 2, 1024], P('req', None, None, 'head')
The draws below stay inside these ranges and needn't reach their ends.
Inputs may be any that keep to these rules, and one draw needn't show every extreme that they name: `lengths`: 0 marks a fresh request.
All inputs are finite; a program needn't handle non-finite values.
Results may differ from the reference program's by a relative error of at most 0.0056.
Values may be sent and summed in bfloat16 or wider, within the bound.
A program may use at most 128 MiB of HBM per device.

```python
import jax
import jax.numpy as jnp
from jax import lax

D = 4096
FF = 21504
HEADS = 128
HEAD_DIM = 64
GROUPS = 8
STATE = 128
CONV = 4
MAX_LEN = 32768
R = 128


def draw_lengths(key, part):
    subkeys = jax.random.split(key, 4)
    categories = jax.random.randint(subkeys[0], (R,), 0, 8)
    long_lengths = jax.random.randint(subkeys[1], (R,), 3, MAX_LEN + 1)
    drawn = jnp.where(categories == 0, 0, jnp.where(categories == 1, 1, jnp.where(categories == 2, 2, long_lengths)))
    first_index = jax.random.randint(subkeys[2], (), 0, R)
    second_index = (first_index + jax.random.randint(subkeys[3], (), 1, R)) % R
    positions = jnp.arange(R)
    drawn = jnp.where(positions == first_index, MAX_LEN, drawn)
    drawn = jnp.where(positions == second_index, 0, drawn)
    return drawn.astype(jnp.int32)


def draw_residual(key, part):
    noise_key, row_key = jax.random.split(key)
    column = jnp.arange(D).astype(jnp.float32) / (D - 1)
    row_scale = jnp.power(10.0, jax.random.uniform(row_key, (R, 1), jnp.float32, -0.5, 0.5))
    noise = jnp.clip(jax.random.normal(noise_key, (R, D), jnp.float32), -6.0, 6.0)
    column_scale = 0.4 * jnp.power(10.0, column)
    return (noise * row_scale * column_scale[None, :]).astype(jnp.bfloat16)


def levels(stream_key, dims, cuts, low, top_value):
    def one(dim, parts):
        steps = jax.random.uniform(jax.random.fold_in(jax.random.fold_in(stream_key, 6), dim), (parts,), jnp.float32, low / len(cuts), top_value / len(cuts))
        return jnp.repeat(jnp.exp(steps), dims[dim] // parts).reshape((-1,) + (1,) * (len(dims) - dim - 1))

    level = one(*cuts[0])
    for cut in cuts[1:]:
        level = level * one(*cut)
    return level


def bell_draw(key, dims, spread, reach, pieces=(), dtype=jnp.bfloat16):
    values = jax.random.normal(key, dims, jnp.float32) * spread
    if len(pieces) > 0:
        values = levels(key, dims, pieces, -0.22, 0.18) * values
    return jnp.clip(values, min=-reach, max=reach).astype(dtype)


def setup_inputs(seed: int = 0) -> dict:
    streams_of = jax.random.split(jax.random.key(seed), 22)
    residual = draw_residual(jax.random.fold_in(streams_of[21], 71), 0)
    lengths = draw_lengths(jax.random.fold_in(streams_of[21], 71), 0)
    ssm_state = bell_draw(streams_of[2], (R, HEADS, HEAD_DIM, STATE), 1.0, 6.0, ((0, 8), (1, 4)), jnp.float32)
    tail_mix = bell_draw(streams_of[3], (R, CONV - 1, HEADS * HEAD_DIM), 1.0, 6.0, ((0, 8), (2, 4)), jnp.float32)
    tail_group = bell_draw(streams_of[4], (R, CONV - 1, 2, GROUPS * STATE), 1.0, 6.0, ((0, 8), (3, 4)), jnp.float32)
    norm_first = jnp.clip(1.0 + 0.18 * jax.random.normal(streams_of[5], (D,), jnp.float32), 0.1, 1.9)
    mix_weight = bell_draw(streams_of[6], (D, 2, HEADS * HEAD_DIM), D ** -0.5, 0.09375, ((0, 8), (2, 4)))
    group_weight = bell_draw(streams_of[7], (D, 2, GROUPS * STATE), D ** -0.5, 0.09375, ((0, 8), (2, 4)))
    step_weight = bell_draw(streams_of[8], (D, HEADS), D ** -0.5, 0.09375, ((0, 8), (1, 4)))
    conv_mix = bell_draw(streams_of[9], (CONV, HEADS * HEAD_DIM), CONV ** -0.5, 3.0, ((1, 4),), jnp.float32)
    conv_group = bell_draw(streams_of[10], (CONV, 2, GROUPS * STATE), CONV ** -0.5, 3.0, ((2, 4),), jnp.float32)
    bias_mix = bell_draw(streams_of[11], (HEADS * HEAD_DIM,), 0.5, 3.0, ((0, 4),), jnp.float32)
    bias_group = bell_draw(streams_of[12], (2, GROUPS * STATE), 0.5, 3.0, ((1, 4),), jnp.float32)
    step_bias = jnp.clip(-2.0 + 3.0 * jax.random.uniform(streams_of[13], (HEADS,), jnp.float32) ** levels(streams_of[13], (HEADS,), ((0, 4),), -0.2, 0.2), -2.0, 1.0)
    decay_log = jnp.clip(-1.0 + 3.0 * jax.random.uniform(streams_of[14], (HEADS,), jnp.float32) ** levels(streams_of[14], (HEADS,), ((0, 4),), -0.2, 0.2), -1.0, 2.0)
    skip_gain = jnp.clip(0.5 + 1.5 * jax.random.uniform(streams_of[15], (HEADS,), jnp.float32) ** levels(streams_of[15], (HEADS,), ((0, 4),), -0.2, 0.2), 0.5, 2.0)
    gate_gain = jnp.clip(1.0 + 0.18 * jax.random.normal(streams_of[16], (HEADS * HEAD_DIM,), jnp.float32), 0.1, 1.9)
    out_weight = bell_draw(streams_of[17], (HEADS * HEAD_DIM, D), (HEADS * HEAD_DIM) ** -0.5, 0.0625, ((0, 4), (1, 8)))
    norm_second = jnp.clip(1.0 + 0.18 * jax.random.normal(streams_of[18], (D,), jnp.float32), 0.1, 1.9)
    up_weight = bell_draw(streams_of[19], (D, FF), D ** -0.5, 0.09375, ((0, 8), (1, 4)))
    down_weight = bell_draw(streams_of[20], (FF, D), FF ** -0.5, 0.0390625, ((0, 4), (1, 8)))
    return dict(residual=residual, lengths=lengths, ssm_state=ssm_state, tail_mix=tail_mix, tail_group=tail_group, norm_first=norm_first, mix_weight=mix_weight, group_weight=group_weight, step_weight=step_weight, conv_mix=conv_mix, conv_group=conv_group, bias_mix=bias_mix, bias_group=bias_group, step_bias=step_bias, decay_log=decay_log, skip_gain=skip_gain, gate_gain=gate_gain, out_weight=out_weight, norm_second=norm_second, up_weight=up_weight, down_weight=down_weight)


eps = 1e-05

def row_inverse(values):
    wide = values.astype(jnp.float32)
    return lax.rsqrt(lax.optimization_barrier(jnp.mean(wide * wide, axis=1, keepdims=True)) + eps)

def reference(residual, lengths, ssm_state, tail_mix, tail_group, norm_first, mix_weight, group_weight, step_weight, conv_mix, conv_group, bias_mix, bias_group, step_bias, decay_log, skip_gain, gate_gain, out_weight, norm_second, up_weight, down_weight):
    inverse_one = row_inverse(residual)
    scaled = (residual.astype(jnp.float32) * norm_first).astype(jnp.bfloat16)
    gate_z = jnp.dot(scaled, mix_weight[:, 0], preferred_element_type=jnp.float32) * inverse_one
    mix_in = jnp.dot(scaled, mix_weight[:, 1], preferred_element_type=jnp.float32) * inverse_one
    group_in = jnp.stack([jnp.dot(scaled, group_weight[:, 0], preferred_element_type=jnp.float32) * inverse_one, jnp.dot(scaled, group_weight[:, 1], preferred_element_type=jnp.float32) * inverse_one], axis=1)
    step_raw = jnp.dot(scaled, step_weight, preferred_element_type=jnp.float32) * inverse_one
    valid = jnp.minimum(lengths, CONV - 1).astype(jnp.int32)
    slots = jnp.arange(CONV - 1).astype(jnp.int32)
    keep = (slots[None, :] >= (CONV - 1 - valid)[:, None]).astype(jnp.float32)
    window_mix = jnp.concatenate([tail_mix * keep[:, :, None], mix_in[:, None, :]], axis=1)
    window_group = jnp.concatenate([tail_group * keep[:, :, None, None], group_in[:, None]], axis=1)
    conv_x = jax.nn.silu(lax.optimization_barrier(jnp.sum(window_mix * conv_mix[None], axis=1)) + bias_mix)
    conv_bc = jax.nn.silu(lax.optimization_barrier(jnp.sum(window_group * conv_group[None], axis=1)) + bias_group)
    step_size = jax.nn.softplus(step_raw + step_bias)
    alive = (lengths > 0).astype(jnp.float32)
    decay = jnp.exp(-step_size * jnp.exp(decay_log)) * alive[:, None]
    per_group = HEADS // GROUPS
    state_parts = []
    output_parts = []
    for group_id in range(GROUPS):
        first_head = group_id * per_group
        prior = ssm_state[:, first_head:first_head + per_group]
        inputs = conv_x[:, first_head * HEAD_DIM:(first_head + per_group) * HEAD_DIM].reshape(R, per_group, HEAD_DIM)
        b_vector = conv_bc[:, 0, group_id * STATE:(group_id + 1) * STATE]
        c_vector = conv_bc[:, 1, group_id * STATE:(group_id + 1) * STATE]
        rate = decay[:, first_head:first_head + per_group]
        stride = step_size[:, first_head:first_head + per_group]
        updated = rate[:, :, None, None] * prior + (stride[:, :, None] * inputs)[..., None] * b_vector[:, None, None, :]
        readout = jnp.einsum('repn,rn->rep', updated, c_vector, precision=lax.Precision.HIGHEST)
        readout = readout + skip_gain[first_head:first_head + per_group][None, :, None] * inputs
        state_parts.append(updated)
        output_parts.append(readout.reshape(R, per_group * HEAD_DIM))
    state_out = jnp.concatenate(state_parts, axis=1)
    mixed = jnp.concatenate(output_parts, axis=1)
    gated = mixed * jax.nn.silu(gate_z)
    grouped = gated.reshape(R, GROUPS, -1)
    inverse = lax.rsqrt(lax.optimization_barrier(jnp.mean(grouped * grouped, axis=2, keepdims=True)) + eps)
    normed_y = ((grouped * inverse).reshape(R, HEADS * HEAD_DIM) * gate_gain).astype(jnp.bfloat16)
    mixer = jnp.dot(normed_y, out_weight, preferred_element_type=jnp.float32)
    middle = (residual.astype(jnp.float32) + mixer).astype(jnp.bfloat16)
    inverse_two = row_inverse(middle)
    scaled_two = (middle.astype(jnp.float32) * norm_second).astype(jnp.bfloat16)
    activation = jnp.dot(scaled_two, up_weight, preferred_element_type=jnp.float32) * inverse_two
    hidden = jnp.square(jax.nn.relu(activation)).astype(jnp.bfloat16)
    projected = jnp.dot(hidden, down_weight, preferred_element_type=jnp.float32)
    residual_out = (middle.astype(jnp.float32) + projected).astype(jnp.bfloat16)
    return (residual_out, state_out, window_mix[:, 1:], window_group[:, 1:])
```

```python
import functools

import jax
import jax.numpy as jnp
from jax import lax
from jax.experimental import pallas as pl
from jax.experimental.pallas import tpu as pltpu
from jax.sharding import PartitionSpec as P

eps = 1e-05
MESH = pl.DeviceIdType.MESH
F32 = jnp.float32
BF16 = jnp.bfloat16
VMEM = pltpu.VMEM


def spans(total, size):
    return [(s, min(size, total - s)) for s in range(0, total, size)]


def remote(src, dst, send, recv, target):
    return pltpu.make_async_remote_copy(
        src_ref=src,
        dst_ref=dst,
        send_sem=send,
        recv_sem=recv,
        device_id=target,
        device_id_type=MESH,
    )


class Place:
    def __init__(self, n_req, n_head):
        self.n_hi = n_req // 2
        self.n_head = n_head
        req = lax.axis_index("req")
        self.head = lax.axis_index("head")
        self.req = req
        self.hi = req // 2
        self.lo = lax.rem(req, 2)
        self.pair = (self.hi * 2 + 1 - self.lo, self.head)

    def hi_at(self, step):
        return lax.rem(self.hi + step + self.n_hi, self.n_hi)

    def column(self, step):
        return (self.hi_at(step) * 2 + self.lo, self.head)

    def head_at(self, step):
        return lax.rem(self.head + step + self.n_head, self.n_head)

    def heads(self, step):
        return (self.req, self.head_at(step))

    def greet(self, with_heads):
        barrier = pltpu.get_barrier_semaphore()
        peers = [self.pair] + [self.column(k) for k in range(1, self.n_hi)]
        if with_heads:
            peers += [self.heads(k) for k in range(1, self.n_head)]
        for peer in peers:
            pl.semaphore_signal(barrier, inc=1, device_id=peer, device_id_type=MESH)
        pl.semaphore_wait(barrier, len(peers))


class Scatter:
    def __init__(self, place, index, cols, part, first, mid, second, sems):
        self.place = place
        self.part, self.first, self.mid, self.second = part, first, mid, second
        self.cols = cols
        pair_send, pair_recv, col_send, col_recv = sems
        n_hi = place.n_hi
        self.to_pair = remote(
            part.at[:, 1 - place.lo, :, cols],
            first.at[:, :, cols],
            pair_send.at[index],
            pair_recv.at[index],
            place.pair,
        )
        self.to_col = [
            remote(
                mid.at[place.hi_at(k), :, cols],
                second.at[k - 1, :, cols],
                col_send.at[index, k - 1],
                col_recv.at[index, k - 1],
                place.column(k),
            )
            for k in range(1, n_hi)
        ]

    def send_pair(self):
        self.to_pair.start()

    def send_column(self):
        place, cols = self.place, self.cols
        self.to_pair.wait_recv()
        for k, copy in enumerate(self.to_col):
            there = place.hi_at(k + 1)
            both = self.part[there, place.lo, :, cols].astype(F32) + self.first[there, :, cols].astype(F32)
            self.mid[there, :, cols] = both.astype(self.mid.dtype)
            copy.start()

    def total(self):
        place, cols = self.place, self.cols
        here = place.hi
        value = self.part[here, place.lo, :, cols].astype(F32) + self.first[here, :, cols].astype(F32)
        for k, copy in enumerate(self.to_col):
            copy.wait_recv()
            value = value + self.second[k, :, cols].astype(F32)
        return value

    def finish(self):
        self.to_pair.wait_send()
        for copy in self.to_col:
            copy.wait_send()


class Gather:
    def __init__(self, place, index, cols, every, sems):
        self.place = place
        col_send, col_recv, pair_send, pair_recv = sems
        n_hi = place.n_hi
        mine = every.at[place.hi, place.lo, :, cols]
        self.to_col = [
            remote(mine, mine, col_send.at[index, k - 1], col_recv.at[index, k - 1], place.column(k))
            for k in range(1, n_hi)
        ]
        self.to_pair = []
        self.from_pair = []
        for k in range(n_hi):
            block = every.at[place.hi_at(-k), place.lo, :, cols]
            self.to_pair.append(remote(block, block, pair_send.at[index, k], pair_recv.at[index, k], place.pair))
            landed = every.at[place.hi_at(-k), 1 - place.lo, :, cols]
            self.from_pair.append(remote(landed, landed, pair_send.at[index, k], pair_recv.at[index, k], place.pair))
        self.from_col = []
        for k in range(1, n_hi):
            block = every.at[place.hi_at(-k), place.lo, :, cols]
            self.from_col.append(
                remote(block, block, col_send.at[index, k - 1], col_recv.at[index, k - 1], place.column(k))
            )

    def send(self):
        for copy in self.to_col:
            copy.start()
        self.to_pair[0].start()

    def forward(self):
        for k, copy in enumerate(self.from_col):
            copy.wait_recv()
            self.to_pair[k + 1].start()

    def land(self):
        for copy in self.from_pair:
            copy.wait_recv()

    def finish(self):
        for copy in self.to_col + self.to_pair:
            copy.wait_send()


def project_kernel(
    n_req, n_head, width_all, chunks, part, squares, out, first, mid, second, first_sq, mid_sq, second_sq,
    pair_send, pair_recv, col_send, col_recv,
):
    place = Place(n_req, n_head)
    place.greet(False)
    sems = (pair_send, pair_recv, col_send, col_recv)
    norm = Scatter(place, len(chunks), slice(None), squares, first_sq, mid_sq, second_sq, sems)
    moves = [
        Scatter(place, c, pl.ds(s, w), part, first, mid, second, sems) for c, (s, w) in enumerate(chunks)
    ]
    norm.send_pair()
    for move in moves:
        move.send_pair()
    norm.send_column()
    inverse = None
    for c in range(len(moves) + 1):
        if c < len(moves):
            moves[c].send_column()
        if c == 0:
            inverse = lax.rsqrt(norm.total()[:, :1] / width_all + eps)
        else:
            s, w = chunks[c - 1]
            out[:, s : s + w] = moves[c - 1].total() * inverse
    norm.finish()
    for move in moves:
        move.finish()


def project(part, squares, n_req, n_head, width_all):
    rows, n = part.shape
    rows_dev = rows // n_req
    n_hi = n_req // 2
    chunks = spans(n, 1024)
    count = len(chunks) + 1
    dma = pltpu.SemaphoreType.DMA
    vmem = pl.BlockSpec(memory_space=VMEM)
    return pl.pallas_call(
        functools.partial(project_kernel, n_req, n_head, width_all, chunks),
        out_shape=jax.ShapeDtypeStruct((rows_dev, n), F32),
        in_specs=[vmem, vmem],
        out_specs=vmem,
        scratch_shapes=[
            VMEM((n_hi, rows_dev, n), BF16),
            VMEM((n_hi, rows_dev, n), BF16),
            VMEM((n_hi - 1, rows_dev, n), BF16),
            VMEM((n_hi, rows_dev, 128), F32),
            VMEM((n_hi, rows_dev, 128), F32),
            VMEM((n_hi - 1, rows_dev, 128), F32),
            dma((count,)),
            dma((count,)),
            dma((count, n_hi - 1)),
            dma((count, n_hi - 1)),
        ],
        compiler_params=pltpu.CompilerParams(
            collective_id=0, has_side_effects=True, vmem_limit_bytes=48 * 1024 * 1024
        ),
    )(part.reshape(n_hi, 2, rows_dev, n), squares.reshape(n_hi, 2, rows_dev, 128))


def state_kernel(groups, per_group, head_dim, decay, stride_t, b_all, c_all, prior, updated, readout, left):
    row = pl.program_id(0)
    rows, state = b_all.shape[0], prior.shape[3]

    @pl.when(row == 0)
    def _():
        wide = stride_t[...]
        high = wide.astype(BF16)
        low = (wide - high.astype(F32)).astype(BF16)
        lane = lax.broadcasted_iota(jnp.int32, wide.shape, 1)
        left[...] = jnp.where(lane < 2 * rows, high.astype(F32), low.astype(F32)).astype(BF16)

    line = lax.broadcasted_iota(jnp.int32, (3 * rows, state), 0)
    chosen = lax.rem(line, rows) == row
    middle = (line >= rows) & (line < 2 * rows)
    own_row = lax.broadcasted_iota(jnp.int32, (rows, state), 0) == row
    span = per_group * head_dim
    for g in range(groups):
        b = b_all[:, g * state : (g + 1) * state]
        b = jnp.concatenate([b, b, b], axis=0)
        b_high = b.astype(BF16).astype(F32)
        b = jnp.where(chosen, jnp.where(middle, b - b_high, b_high), 0.0).astype(BF16)
        c = c_all[:, g * state : (g + 1) * state]
        c = jnp.sum(jnp.where(own_row, c, 0.0), axis=0, keepdims=True)
        c_high = c.astype(BF16).astype(F32)
        place = lax.broadcasted_iota(jnp.int32, (16, state), 0)
        c = jnp.where(place == 0, c_high, jnp.where(place == 1, c - c_high, 0.0)).astype(BF16)
        outer = jnp.dot(left[g * span : (g + 1) * span, :], b, preferred_element_type=F32)
        pieces = []
        for e in range(per_group):
            h = g * per_group + e
            value = decay[row, h] * prior[0, h] + outer[e * head_dim : (e + 1) * head_dim]
            updated[0, h] = value
            pieces.append(value.astype(BF16))
        block = jnp.concatenate(pieces, axis=0)
        found = lax.dot_general(c, block, (((1,), (1,)), ((), ())), preferred_element_type=F32)
        readout[0, :, g * span : (g + 1) * span] = jnp.sum(found, axis=0, keepdims=True)


def state_step(decay, stride, b_vector, c_vector, prior):
    rows, heads, head_dim, state = prior.shape
    groups = b_vector.shape[1] // state
    turned = stride.T
    vmem = pl.BlockSpec(memory_space=VMEM)
    block = pl.BlockSpec((1, heads, head_dim, state), lambda r: (r, 0, 0, 0))
    mix = heads * head_dim
    updated, readout = pl.pallas_call(
        functools.partial(state_kernel, groups, heads // groups, head_dim),
        grid=(rows,),
        out_shape=(
            jax.ShapeDtypeStruct(prior.shape, F32),
            jax.ShapeDtypeStruct((rows, 1, mix), F32),
        ),
        in_specs=[pl.BlockSpec(memory_space=pltpu.SMEM), vmem, vmem, vmem, block],
        out_specs=(block, pl.BlockSpec((1, 1, mix), lambda r: (r, 0, 0))),
        scratch_shapes=[VMEM((mix, 3 * rows), BF16)],
        compiler_params=pltpu.CompilerParams(vmem_limit_bytes=48 * 1024 * 1024),
        cost_estimate=pl.CostEstimate(flops=4 * prior.size * 48, bytes_accessed=8 * prior.size, transcendentals=0),
    )(decay, jnp.concatenate([turned, turned, turned], axis=1), b_vector, c_vector, prior)
    return updated, readout.reshape(rows, mix)


def mlp_kernel(
    n_req, n_head, width_all, y_chunks, chunks,
    residual, y_own, gain, out_w, up_w, down_w, out,
    out_v, up_v, down_v, y_all, partial, partial_in, mid_all, act, first, mid, second,
    squares, first_sq, mid_sq, second_sq, hidden, result,
    load, y_cs, y_cr, y_ps, y_pr, h_send, h_recv, g_send, g_recv,
    s_ps, s_pr, s_cs, s_cr, a_cs, a_cr, a_ps, a_pr, h2_send, h2_recv, g2_send, g2_recv,
):
    loads = [
        pltpu.make_async_copy(src, dst, load.at[i])
        for i, (src, dst) in enumerate([(out_w, out_v), (up_w, up_v), (down_w, down_v)])
    ]
    for copy in loads:
        copy.start()
    place = Place(n_req, n_head)
    place.greet(True)
    n_hi = place.n_hi
    rows = residual.shape[0]
    width = residual.shape[1]
    rows_dev = rows // n_req
    rows_head = rows // n_head
    at_head = pl.multiple_of(place.head * rows_head, rows_head)

    def spread(send_from, land_in, send, recv):
        copies = []
        for k in range(1, n_head):
            copies.append(
                remote(
                    send_from(place.head_at(k)), land_in(k), send.at[k - 1], recv.at[k - 1], place.heads(k)
                )
            )
            copies[-1].start()
        return copies

    def block_of(ref, index):
        return ref.at[pl.ds(pl.multiple_of(index * rows_head, rows_head), rows_head)]

    def head_sum(send, recv, landing):
        copies = spread(lambda h: block_of(partial, h), lambda k: landing.at[k - 1], send, recv)
        total = partial[pl.ds(at_head, rows_head), :].astype(F32)
        for k, copy in enumerate(copies):
            copy.wait_recv()
            total = total + landing[k].astype(F32)
        return total, copies

    def head_gather(ref, send, recv):
        mine = block_of(ref, place.head)
        copies = spread(lambda h: mine, lambda k: mine, send, recv)
        for k in range(1, n_head):
            there = block_of(ref, place.head_at(-k))
            remote(there, there, send.at[k - 1], recv.at[k - 1], place.heads(k)).wait_recv()
        return copies

    pending = []
    y_all[place.hi, place.lo] = y_own[...]
    gathers = [
        Gather(place, c, pl.ds(s, w), y_all, (y_cs, y_cr, y_ps, y_pr)) for c, (s, w) in enumerate(y_chunks)
    ]
    for move in gathers:
        move.send()
    for move in gathers:
        move.forward()
    loads[0].wait()
    mixer = None
    for move, (s, w) in zip(gathers, y_chunks):
        move.land()
        term = jnp.dot(
            y_all[:, :, :, s : s + w].reshape(rows, w), out_v[s : s + w, :], preferred_element_type=F32
        )
        mixer = term if mixer is None else mixer + term
    partial[...] = mixer.astype(BF16)
    total, copies = head_sum(h_send, h_recv, partial_in.at[0])
    pending += gathers
    for copy in copies:
        copy.wait_send()
    mid_all[pl.ds(at_head, rows_head), :] = (
        residual[pl.ds(at_head, rows_head), :].astype(F32) + total
    ).astype(BF16)
    copies = head_gather(mid_all, g_send, g_recv)
    for copy in copies:
        copy.wait_send()

    wide = mid_all[...].astype(F32)
    sums = jnp.sum(wide * wide, axis=1, keepdims=True)
    squares[...] = jnp.broadcast_to(sums, (rows, 128)).reshape(n_hi, 2, rows_dev, 128)
    sems = (s_ps, s_pr, s_cs, s_cr)
    norm = Scatter(place, len(chunks), slice(None), squares, first_sq, mid_sq, second_sq, sems)
    norm.send_pair()
    scaled = (wide * gain[...]).astype(BF16)
    moves = []
    shares = []
    loads[1].wait()
    for c, (s, w) in enumerate(chunks):
        piece = jnp.dot(scaled, up_v[:, s : s + w], preferred_element_type=F32).astype(BF16)
        act[:, :, :, s : s + w] = piece.reshape(n_hi, 2, rows_dev, w)
        moves.append(Scatter(place, c, pl.ds(s, w), act, first, mid, second, sems))
        moves[-1].send_pair()
        shares.append(Gather(place, c, pl.ds(s, w), hidden, (a_cs, a_cr, a_ps, a_pr)))
    norm.send_column()
    loads[2].wait()
    count = len(chunks)
    inverse = None
    projected = None
    for step in range(count + 3):
        if step < count:
            moves[step].send_column()
        c = step - 1
        if 0 <= c < count:
            if inverse is None:
                inverse = lax.rsqrt(norm.total()[:, :1] / width_all + eps)
            s, w = chunks[c]
            share = jnp.maximum(moves[c].total() * inverse, 0.0)
            hidden[place.hi, place.lo, :, pl.ds(s, w)] = (share * share).astype(BF16)
            shares[c].send()
        c = step - 2
        if 0 <= c < count:
            shares[c].forward()
        c = step - 3
        if 0 <= c < count:
            shares[c].land()
            s, w = chunks[c]
            term = jnp.dot(
                hidden[:, :, :, s : s + w].reshape(rows, w), down_v[s : s + w, :], preferred_element_type=F32
            )
            projected = term if projected is None else projected + term
    partial[...] = projected.astype(BF16)
    total, copies = head_sum(h2_send, h2_recv, partial_in.at[1])
    for copy in copies:
        copy.wait_send()
    result[pl.ds(at_head, rows_head), :] = (
        mid_all[pl.ds(at_head, rows_head), :].astype(F32) + total
    ).astype(BF16)
    copies = head_gather(result, g2_send, g2_recv)
    out[...] = result[...]
    for copy in copies:
        copy.wait_send()
    norm.finish()
    for move in pending + moves + shares:
        move.finish()


def mlp(residual, y_own, gain, out_w, up_w, down_w, n_req, n_head, width_all):
    rows, width = residual.shape
    rows_dev, mix = y_own.shape
    ff = up_w.shape[1]
    n_hi = n_req // 2
    y_chunks = spans(mix, 1024)
    chunks = spans(ff, 896)
    count, y_count = len(chunks), len(y_chunks)
    rows_head = rows // n_head
    dma = pltpu.SemaphoreType.DMA
    vmem = pl.BlockSpec(memory_space=VMEM)
    anywhere = pl.BlockSpec(memory_space=pl.ANY)
    n_col, n_side = n_hi - 1, n_head - 1
    return pl.pallas_call(
        functools.partial(mlp_kernel, n_req, n_head, width_all, y_chunks, chunks),
        out_shape=jax.ShapeDtypeStruct((rows, width), BF16),
        in_specs=[vmem, vmem, vmem, anywhere, anywhere, anywhere],
        out_specs=vmem,
        scratch_shapes=[
            VMEM(out_w.shape, BF16),
            VMEM(up_w.shape, BF16),
            VMEM(down_w.shape, BF16),
            VMEM((n_hi, 2, rows_dev, mix), BF16),
            VMEM((rows, width), BF16),
            VMEM((2, n_side, rows_head, width), BF16),
            VMEM((rows, width), BF16),
            VMEM((n_hi, 2, rows_dev, ff), BF16),
            VMEM((n_hi, rows_dev, ff), BF16),
            VMEM((n_hi, rows_dev, ff), BF16),
            VMEM((n_col, rows_dev, ff), BF16),
            VMEM((n_hi, 2, rows_dev, 128), F32),
            VMEM((n_hi, rows_dev, 128), F32),
            VMEM((n_hi, rows_dev, 128), F32),
            VMEM((n_col, rows_dev, 128), F32),
            VMEM((n_hi, 2, rows_dev, ff), BF16),
            VMEM((rows, width), BF16),
            dma((3,)),
            dma((y_count, n_col)),
            dma((y_count, n_col)),
            dma((y_count, n_hi)),
            dma((y_count, n_hi)),
            dma((n_side,)),
            dma((n_side,)),
            dma((n_side,)),
            dma((n_side,)),
            dma((count + 1,)),
            dma((count + 1,)),
            dma((count + 1, n_col)),
            dma((count + 1, n_col)),
            dma((count, n_col)),
            dma((count, n_col)),
            dma((count, n_hi)),
            dma((count, n_hi)),
            dma((n_side,)),
            dma((n_side,)),
            dma((n_side,)),
            dma((n_side,)),
        ],
        compiler_params=pltpu.CompilerParams(
            collective_id=1, has_side_effects=True, vmem_limit_bytes=52 * 1024 * 1024
        ),
    )(residual, y_own, gain.reshape(1, width), out_w, up_w, down_w)


def on_device(
    residual,
    lengths,
    ssm_state,
    tail_mix,
    tail_group,
    norm_first,
    mix_weight,
    group_weight,
    step_weight,
    conv_mix,
    conv_group,
    bias_mix,
    bias_group,
    step_bias,
    decay_log,
    skip_gain,
    gate_gain,
    out_weight,
    norm_second,
    up_weight,
    down_weight,
):
    rows_dev, heads_dev, head_dim, state_size = ssm_state.shape
    mix_dev = mix_weight.shape[2]
    group_dev = group_weight.shape[2]
    groups_dev = group_dev // state_size
    rows, width_dev = residual.shape
    n_req, n_head = lax.axis_size("req"), lax.axis_size("head")
    width_all = width_dev * n_req
    taps_all = conv_mix.shape[0]
    wide = residual.astype(F32)
    squares = jnp.broadcast_to(jnp.sum(wide * wide, axis=1, keepdims=True), (rows, 128))
    scaled = (wide * norm_first).astype(BF16)
    steps_pad = -heads_dev % 128
    pieces = [
        jnp.dot(scaled, mix_weight[:, 0], preferred_element_type=F32),
        jnp.dot(scaled, mix_weight[:, 1], preferred_element_type=F32),
        jnp.dot(scaled, group_weight[:, 0], preferred_element_type=F32),
        jnp.dot(scaled, group_weight[:, 1], preferred_element_type=F32),
        jnp.pad(jnp.dot(scaled, step_weight, preferred_element_type=F32), ((0, 0), (0, steps_pad))),
    ]
    part = jnp.concatenate([piece.astype(BF16) for piece in pieces], axis=1)
    sums = project(part, squares, n_req, n_head, width_all)
    gate_z = sums[:, :mix_dev]
    mix_in = sums[:, mix_dev : 2 * mix_dev]
    group_in = sums[:, 2 * mix_dev : 2 * mix_dev + 2 * group_dev].reshape(rows_dev, 2, group_dev)
    step_raw = sums[:, 2 * mix_dev + 2 * group_dev : 2 * mix_dev + 2 * group_dev + heads_dev]
    valid = jnp.minimum(lengths, taps_all - 1)
    slots = jnp.arange(taps_all - 1)
    keep = (slots[None, :] >= (taps_all - 1 - valid)[:, None]).astype(F32)
    window_mix = jnp.concatenate([tail_mix * keep[:, :, None], mix_in[:, None, :]], axis=1)
    window_group = jnp.concatenate([tail_group * keep[:, :, None, None], group_in[:, None]], axis=1)
    conv_x = jax.nn.silu(jnp.sum(window_mix * conv_mix[None], axis=1) + bias_mix)
    conv_bc = jax.nn.silu(jnp.sum(window_group * conv_group[None], axis=1) + bias_group)
    step_size = jax.nn.softplus(step_raw + step_bias)
    alive = (lengths > 0).astype(F32)
    decay = jnp.exp(-step_size * jnp.exp(decay_log)) * alive[:, None]
    stride = jnp.repeat(step_size, head_dim, axis=1) * conv_x
    state_out, readout = state_step(decay, stride, conv_bc[:, 0], conv_bc[:, 1], ssm_state)
    mixed = readout + jnp.repeat(skip_gain, head_dim)[None, :] * conv_x
    gated = mixed * jax.nn.silu(gate_z)
    grouped = gated.reshape(rows_dev, groups_dev, -1)
    inverse = lax.rsqrt(jnp.mean(grouped * grouped, axis=2, keepdims=True) + eps)
    normed_y = ((grouped * inverse).reshape(rows_dev, mix_dev) * gate_gain).astype(BF16)
    residual_out = mlp(
        residual, normed_y, norm_second, out_weight, up_weight, down_weight, n_req, n_head, width_all
    )
    return (residual_out, state_out, window_mix[:, 1:], window_group[:, 1:])


def solution(mesh):
    return jax.shard_map(
        on_device,
        mesh=mesh,
        in_specs=(
            P(None, "req"),
            P("req"),
            P("req", "head", None, None),
            P("req", None, "head"),
            P("req", None, None, "head"),
            P("req"),
            P("req", None, "head"),
            P("req", None, "head"),
            P("req", "head"),
            P(None, "head"),
            P(None, None, "head"),
            P("head"),
            P(None, "head"),
            P("head"),
            P("head"),
            P("head"),
            P("head"),
            P("head", "req"),
            P("req"),
            P("req", "head"),
            P("head", "req"),
        ),
        out_specs=(
            P(None, "req"),
            P("req", "head", None, None),
            P("req", None, "head"),
            P("req", None, None, "head"),
        ),
        check_vma=False,
    )
```

```python
import functools

import jax
import jax.numpy as jnp
from jax import lax
from jax.experimental import pallas as pl
from jax.experimental.pallas import tpu as pltpu
from jax.sharding import PartitionSpec as P

eps = 1e-05
MESH = pl.DeviceIdType.MESH
F32 = jnp.float32
BF16 = jnp.bfloat16
VMEM = pltpu.VMEM


def spans(total, size):
    return [(s, min(size, total - s)) for s in range(0, total, size)]


def remote(src, dst, send, recv, target):
    return pltpu.make_async_remote_copy(
        src_ref=src,
        dst_ref=dst,
        send_sem=send,
        recv_sem=recv,
        device_id=target,
        device_id_type=MESH,
    )


class Place:
    def __init__(self, n_req, n_head):
        self.n_hi = n_req // 2
        self.n_head = n_head
        req = lax.axis_index("req")
        self.head = lax.axis_index("head")
        self.req = req
        self.hi = req // 2
        self.lo = lax.rem(req, 2)
        self.pair = (self.hi * 2 + 1 - self.lo, self.head)

    def hi_at(self, step):
        return lax.rem(self.hi + step + self.n_hi, self.n_hi)

    def column(self, step):
        return (self.hi_at(step) * 2 + self.lo, self.head)

    def head_at(self, step):
        return lax.rem(self.head + step + self.n_head, self.n_head)

    def heads(self, step):
        return (self.req, self.head_at(step))

    def greet(self, with_heads):
        barrier = pltpu.get_barrier_semaphore()
        peers = [self.pair] + [self.column(k) for k in range(1, self.n_hi)]
        if with_heads:
            peers += [self.heads(k) for k in range(1, self.n_head)]
        for peer in peers:
            pl.semaphore_signal(barrier, inc=1, device_id=peer, device_id_type=MESH)
        pl.semaphore_wait(barrier, len(peers))


class Scatter:
    def __init__(self, place, index, cols, part, first, mid, second, sems):
        self.place = place
        self.part, self.first, self.mid, self.second = part, first, mid, second
        self.cols = cols
        pair_send, pair_recv, col_send, col_recv = sems
        n_hi = place.n_hi
        self.to_pair = remote(
            part.at[:, 1 - place.lo, :, cols],
            first.at[:, :, cols],
            pair_send.at[index],
            pair_recv.at[index],
            place.pair,
        )
        self.to_col = [
            remote(
                mid.at[place.hi_at(k), :, cols],
                second.at[k - 1, :, cols],
                col_send.at[index, k - 1],
                col_recv.at[index, k - 1],
                place.column(k),
            )
            for k in range(1, n_hi)
        ]

    def send_pair(self):
        self.to_pair.start()

    def send_column(self):
        place, cols = self.place, self.cols
        self.to_pair.wait_recv()
        for k, copy in enumerate(self.to_col):
            there = place.hi_at(k + 1)
            both = self.part[there, place.lo, :, cols].astype(F32) + self.first[there, :, cols].astype(F32)
            self.mid[there, :, cols] = both.astype(self.mid.dtype)
            copy.start()

    def total(self):
        place, cols = self.place, self.cols
        here = place.hi
        value = self.part[here, place.lo, :, cols].astype(F32) + self.first[here, :, cols].astype(F32)
        for k, copy in enumerate(self.to_col):
            copy.wait_recv()
            value = value + self.second[k, :, cols].astype(F32)
        return value

    def finish(self):
        self.to_pair.wait_send()
        for copy in self.to_col:
            copy.wait_send()


class Gather:
    def __init__(self, place, index, cols, every, sems):
        self.place = place
        col_send, col_recv, pair_send, pair_recv = sems
        n_hi = place.n_hi
        mine = every.at[place.hi, place.lo, :, cols]
        self.to_col = [
            remote(mine, mine, col_send.at[index, k - 1], col_recv.at[index, k - 1], place.column(k))
            for k in range(1, n_hi)
        ]
        self.to_pair = []
        self.from_pair = []
        for k in range(n_hi):
            block = every.at[place.hi_at(-k), place.lo, :, cols]
            self.to_pair.append(remote(block, block, pair_send.at[index, k], pair_recv.at[index, k], place.pair))
            landed = every.at[place.hi_at(-k), 1 - place.lo, :, cols]
            self.from_pair.append(remote(landed, landed, pair_send.at[index, k], pair_recv.at[index, k], place.pair))
        self.from_col = []
        for k in range(1, n_hi):
            block = every.at[place.hi_at(-k), place.lo, :, cols]
            self.from_col.append(
                remote(block, block, col_send.at[index, k - 1], col_recv.at[index, k - 1], place.column(k))
            )

    def send(self):
        for copy in self.to_col:
            copy.start()
        self.to_pair[0].start()

    def forward(self):
        for k, copy in enumerate(self.from_col):
            copy.wait_recv()
            self.to_pair[k + 1].start()

    def land(self):
        for copy in self.from_pair:
            copy.wait_recv()

    def finish(self):
        for copy in self.to_col + self.to_pair:
            copy.wait_send()


def project_kernel(
    n_req, n_head, width_all, chunks, residual, gain, mix_w, group_w, step_w, out,
    part, first, mid, second, squares, first_sq, mid_sq, second_sq,
    pair_send, pair_recv, col_send, col_recv,
):
    place = Place(n_req, n_head)
    place.greet(False)
    sems = (pair_send, pair_recv, col_send, col_recv)
    n_hi = place.n_hi
    rows = residual.shape[0]
    rows_dev = rows // n_req
    wide = residual[...].astype(F32)
    sums = jnp.sum(wide * wide, axis=1, keepdims=True)
    squares[...] = jnp.broadcast_to(sums, (rows, 128)).reshape(n_hi, 2, rows_dev, 128)
    norm = Scatter(place, len(chunks), slice(None), squares, first_sq, mid_sq, second_sq, sems)
    norm.send_pair()
    scaled = (wide * gain[...]).astype(BF16)
    mix = mix_w.shape[1]
    moves = []
    for c, (s, w) in enumerate(chunks):
        if s < mix:
            product = jnp.dot(scaled, mix_w[:, s : s + w], preferred_element_type=F32)
        else:
            product = jnp.concatenate(
                [
                    jnp.dot(scaled, group_w[...], preferred_element_type=F32),
                    jnp.dot(scaled, step_w[...], preferred_element_type=F32),
                ],
                axis=1,
            )
        part[:, :, :, s : s + w] = product.astype(BF16).reshape(n_hi, 2, rows_dev, w)
        moves.append(Scatter(place, c, pl.ds(s, w), part, first, mid, second, sems))
        moves[-1].send_pair()
    norm.send_column()
    inverse = None
    for c in range(len(moves) + 1):
        if c < len(moves):
            moves[c].send_column()
        if c == 0:
            inverse = lax.rsqrt(norm.total()[:, :1] / width_all + eps)
        else:
            s, w = chunks[c - 1]
            out[:, s : s + w] = moves[c - 1].total() * inverse
    norm.finish()
    for move in moves:
        move.finish()


def project(residual, gain, mix_w, group_w, step_w, n_req, n_head, width_all):
    rows, width = residual.shape
    mix, rest = mix_w.shape[1], group_w.shape[1] + step_w.shape[1]
    n = mix + rest
    rows_dev = rows // n_req
    n_hi = n_req // 2
    chunks = spans(mix, 1024) + [(mix, rest)]
    count = len(chunks) + 1
    dma = pltpu.SemaphoreType.DMA
    vmem = pl.BlockSpec(memory_space=VMEM)
    return pl.pallas_call(
        functools.partial(project_kernel, n_req, n_head, width_all, chunks),
        out_shape=jax.ShapeDtypeStruct((rows_dev, n), F32),
        in_specs=[vmem] * 5,
        out_specs=vmem,
        scratch_shapes=[
            VMEM((n_hi, 2, rows_dev, n), BF16),
            VMEM((n_hi, rows_dev, n), BF16),
            VMEM((n_hi, rows_dev, n), BF16),
            VMEM((n_hi - 1, rows_dev, n), BF16),
            VMEM((n_hi, 2, rows_dev, 128), F32),
            VMEM((n_hi, rows_dev, 128), F32),
            VMEM((n_hi, rows_dev, 128), F32),
            VMEM((n_hi - 1, rows_dev, 128), F32),
            dma((count,)),
            dma((count,)),
            dma((count, n_hi - 1)),
            dma((count, n_hi - 1)),
        ],
        compiler_params=pltpu.CompilerParams(
            collective_id=0, has_side_effects=True, vmem_limit_bytes=32 * 1024 * 1024
        ),
    )(residual, gain.reshape(1, width), mix_w, group_w, step_w)


def state_kernel(batch, groups, per_group, head_dim, decay, stride_t, b_all, c_all, prior, updated, readout, left):
    turn = pl.program_id(0)
    rows, state = b_all.shape[0], prior.shape[3]

    @pl.when(turn == 0)
    def _():
        wide = stride_t[...]
        high = wide.astype(BF16)
        low = (wide - high.astype(F32)).astype(BF16)
        lane = lax.broadcasted_iota(jnp.int32, wide.shape, 1)
        left[...] = jnp.where(lane < 2 * rows, high.astype(F32), low.astype(F32)).astype(BF16)

    line = lax.broadcasted_iota(jnp.int32, (3 * rows, state), 0)
    middle = (line >= rows) & (line < 2 * rows)
    span = per_group * head_dim
    for i in range(batch):
        row = turn * batch + i
        chosen = lax.rem(line, rows) == row
        own_row = lax.broadcasted_iota(jnp.int32, (rows, state), 0) == row
        for g in range(groups):
            b = b_all[:, g * state : (g + 1) * state]
            b = jnp.concatenate([b, b, b], axis=0)
            b_high = b.astype(BF16).astype(F32)
            b = jnp.where(chosen, jnp.where(middle, b - b_high, b_high), 0.0).astype(BF16)
            c = c_all[:, g * state : (g + 1) * state]
            c = jnp.sum(jnp.where(own_row, c, 0.0), axis=0, keepdims=True)
            c_high = c.astype(BF16).astype(F32)
            place = lax.broadcasted_iota(jnp.int32, (16, state), 0)
            c = jnp.where(place == 0, c_high, jnp.where(place == 1, c - c_high, 0.0)).astype(BF16)
            outer = jnp.dot(left[g * span : (g + 1) * span, :], b, preferred_element_type=F32)
            pieces = []
            for e in range(per_group):
                h = g * per_group + e
                value = decay[row, h] * prior[i, h] + outer[e * head_dim : (e + 1) * head_dim]
                updated[i, h] = value
                pieces.append(value.astype(BF16))
            block = jnp.concatenate(pieces, axis=0)
            found = lax.dot_general(c, block, (((1,), (1,)), ((), ())), preferred_element_type=F32)
            readout[i, :, g * span : (g + 1) * span] = jnp.sum(found, axis=0, keepdims=True)


def state_step(decay, stride, b_vector, c_vector, prior):
    rows, heads, head_dim, state = prior.shape
    groups = b_vector.shape[1] // state
    turned = stride.T
    vmem = pl.BlockSpec(memory_space=VMEM)
    batch = 2 if rows % 2 == 0 else 1
    block = pl.BlockSpec((batch, heads, head_dim, state), lambda r: (r, 0, 0, 0))
    mix = heads * head_dim
    updated, readout = pl.pallas_call(
        functools.partial(state_kernel, batch, groups, heads // groups, head_dim),
        grid=(rows // batch,),
        out_shape=(
            jax.ShapeDtypeStruct(prior.shape, F32),
            jax.ShapeDtypeStruct((rows, 1, mix), F32),
        ),
        in_specs=[pl.BlockSpec(memory_space=pltpu.SMEM), vmem, vmem, vmem, block],
        out_specs=(block, pl.BlockSpec((batch, 1, mix), lambda r: (r, 0, 0))),
        scratch_shapes=[VMEM((mix, 3 * rows), BF16)],
        compiler_params=pltpu.CompilerParams(vmem_limit_bytes=48 * 1024 * 1024),
        cost_estimate=pl.CostEstimate(flops=4 * prior.size * 48, bytes_accessed=8 * prior.size, transcendentals=0),
    )(decay, jnp.concatenate([turned, turned, turned], axis=1), b_vector, c_vector, prior)
    return updated, readout.reshape(rows, mix)


def mlp_kernel(
    n_req, n_head, width_all, y_chunks, chunks,
    residual, y_own, gain, out_w, up_w, down_w, out,
    out_v, up_v, down_v, y_all, partial, partial_in, mid_all, act, first, mid, second,
    squares, first_sq, mid_sq, second_sq, hidden, result,
    load, y_cs, y_cr, y_ps, y_pr, h_send, h_recv, g_send, g_recv,
    s_ps, s_pr, s_cs, s_cr, a_cs, a_cr, a_ps, a_pr, h2_send, h2_recv, g2_send, g2_recv,
):
    loads = [
        pltpu.make_async_copy(src, dst, load.at[i])
        for i, (src, dst) in enumerate([(out_w, out_v), (up_w, up_v), (down_w, down_v)])
    ]
    for copy in loads:
        copy.start()
    place = Place(n_req, n_head)
    place.greet(True)
    n_hi = place.n_hi
    rows = residual.shape[0]
    width = residual.shape[1]
    rows_dev = rows // n_req
    rows_head = rows // n_head
    at_head = pl.multiple_of(place.head * rows_head, rows_head)

    def spread(send_from, land_in, send, recv):
        copies = []
        for k in range(1, n_head):
            copies.append(
                remote(
                    send_from(place.head_at(k)), land_in(k), send.at[k - 1], recv.at[k - 1], place.heads(k)
                )
            )
            copies[-1].start()
        return copies

    def block_of(ref, index):
        return ref.at[pl.ds(pl.multiple_of(index * rows_head, rows_head), rows_head)]

    def head_sum(send, recv, landing):
        copies = spread(lambda h: block_of(partial, h), lambda k: landing.at[k - 1], send, recv)
        total = partial[pl.ds(at_head, rows_head), :].astype(F32)
        for k, copy in enumerate(copies):
            copy.wait_recv()
            total = total + landing[k].astype(F32)
        return total, copies

    def head_gather(ref, send, recv):
        mine = block_of(ref, place.head)
        copies = spread(lambda h: mine, lambda k: mine, send, recv)
        for k in range(1, n_head):
            there = block_of(ref, place.head_at(-k))
            remote(there, there, send.at[k - 1], recv.at[k - 1], place.heads(k)).wait_recv()
        return copies

    pending = []
    y_all[place.hi, place.lo] = y_own[...]
    gathers = [
        Gather(place, c, pl.ds(s, w), y_all, (y_cs, y_cr, y_ps, y_pr)) for c, (s, w) in enumerate(y_chunks)
    ]
    for move in gathers:
        move.send()
    for move in gathers:
        move.forward()
    loads[0].wait()
    mixer = None
    for move, (s, w) in zip(gathers, y_chunks):
        move.land()
        term = jnp.dot(
            y_all[:, :, :, s : s + w].reshape(rows, w), out_v[s : s + w, :], preferred_element_type=F32
        )
        mixer = term if mixer is None else mixer + term
    partial[...] = mixer.astype(BF16)
    total, copies = head_sum(h_send, h_recv, partial_in.at[0])
    pending += gathers
    for copy in copies:
        copy.wait_send()
    mid_all[pl.ds(at_head, rows_head), :] = (
        residual[pl.ds(at_head, rows_head), :].astype(F32) + total
    ).astype(BF16)
    copies = head_gather(mid_all, g_send, g_recv)
    for copy in copies:
        copy.wait_send()

    wide = mid_all[...].astype(F32)
    sums = jnp.sum(wide * wide, axis=1, keepdims=True)
    squares[...] = jnp.broadcast_to(sums, (rows, 128)).reshape(n_hi, 2, rows_dev, 128)
    sems = (s_ps, s_pr, s_cs, s_cr)
    norm = Scatter(place, len(chunks), slice(None), squares, first_sq, mid_sq, second_sq, sems)
    norm.send_pair()
    scaled = (wide * gain[...]).astype(BF16)
    moves = []
    shares = []
    loads[1].wait()
    for c, (s, w) in enumerate(chunks):
        piece = jnp.dot(scaled, up_v[:, s : s + w], preferred_element_type=F32).astype(BF16)
        act[:, :, :, s : s + w] = piece.reshape(n_hi, 2, rows_dev, w)
        moves.append(Scatter(place, c, pl.ds(s, w), act, first, mid, second, sems))
        moves[-1].send_pair()
        shares.append(Gather(place, c, pl.ds(s, w), hidden, (a_cs, a_cr, a_ps, a_pr)))
    norm.send_column()
    loads[2].wait()
    count = len(chunks)
    inverse = None
    projected = None
    for step in range(count + 3):
        if step < count:
            moves[step].send_column()
        c = step - 1
        if 0 <= c < count:
            if inverse is None:
                inverse = lax.rsqrt(norm.total()[:, :1] / width_all + eps)
            s, w = chunks[c]
            share = jnp.maximum(moves[c].total() * inverse, 0.0)
            hidden[place.hi, place.lo, :, pl.ds(s, w)] = (share * share).astype(BF16)
            shares[c].send()
        c = step - 2
        if 0 <= c < count:
            shares[c].forward()
        c = step - 3
        if 0 <= c < count:
            shares[c].land()
            s, w = chunks[c]
            term = jnp.dot(
                hidden[:, :, :, s : s + w].reshape(rows, w), down_v[s : s + w, :], preferred_element_type=F32
            )
            projected = term if projected is None else projected + term
    partial[...] = projected.astype(BF16)
    total, copies = head_sum(h2_send, h2_recv, partial_in.at[1])
    for copy in copies:
        copy.wait_send()
    result[pl.ds(at_head, rows_head), :] = (
        mid_all[pl.ds(at_head, rows_head), :].astype(F32) + total
    ).astype(BF16)
    copies = head_gather(result, g2_send, g2_recv)
    out[...] = result[...]
    for copy in copies:
        copy.wait_send()
    norm.finish()
    for move in pending + moves + shares:
        move.finish()


def mlp(residual, y_own, gain, out_w, up_w, down_w, n_req, n_head, width_all):
    rows, width = residual.shape
    rows_dev, mix = y_own.shape
    ff = up_w.shape[1]
    n_hi = n_req // 2
    y_chunks = spans(mix, 1024)
    chunks = spans(ff, 896)
    count, y_count = len(chunks), len(y_chunks)
    rows_head = rows // n_head
    dma = pltpu.SemaphoreType.DMA
    vmem = pl.BlockSpec(memory_space=VMEM)
    anywhere = pl.BlockSpec(memory_space=pl.ANY)
    n_col, n_side = n_hi - 1, n_head - 1
    return pl.pallas_call(
        functools.partial(mlp_kernel, n_req, n_head, width_all, y_chunks, chunks),
        out_shape=jax.ShapeDtypeStruct((rows, width), BF16),
        in_specs=[vmem, vmem, vmem, anywhere, anywhere, anywhere],
        out_specs=vmem,
        scratch_shapes=[
            VMEM(out_w.shape, BF16),
            VMEM(up_w.shape, BF16),
            VMEM(down_w.shape, BF16),
            VMEM((n_hi, 2, rows_dev, mix), BF16),
            VMEM((rows, width), BF16),
            VMEM((2, n_side, rows_head, width), BF16),
            VMEM((rows, width), BF16),
            VMEM((n_hi, 2, rows_dev, ff), BF16),
            VMEM((n_hi, rows_dev, ff), BF16),
            VMEM((n_hi, rows_dev, ff), BF16),
            VMEM((n_col, rows_dev, ff), BF16),
            VMEM((n_hi, 2, rows_dev, 128), F32),
            VMEM((n_hi, rows_dev, 128), F32),
            VMEM((n_hi, rows_dev, 128), F32),
            VMEM((n_col, rows_dev, 128), F32),
            VMEM((n_hi, 2, rows_dev, ff), BF16),
            VMEM((rows, width), BF16),
            dma((3,)),
            dma((y_count, n_col)),
            dma((y_count, n_col)),
            dma((y_count, n_hi)),
            dma((y_count, n_hi)),
            dma((n_side,)),
            dma((n_side,)),
            dma((n_side,)),
            dma((n_side,)),
            dma((count + 1,)),
            dma((count + 1,)),
            dma((count + 1, n_col)),
            dma((count + 1, n_col)),
            dma((count, n_col)),
            dma((count, n_col)),
            dma((count, n_hi)),
            dma((count, n_hi)),
            dma((n_side,)),
            dma((n_side,)),
            dma((n_side,)),
            dma((n_side,)),
        ],
        compiler_params=pltpu.CompilerParams(
            collective_id=1, has_side_effects=True, vmem_limit_bytes=52 * 1024 * 1024
        ),
    )(residual, y_own, gain.reshape(1, width), out_w, up_w, down_w)


def on_device(
    residual,
    lengths,
    ssm_state,
    tail_mix,
    tail_group,
    norm_first,
    mix_weight,
    group_weight,
    step_weight,
    conv_mix,
    conv_group,
    bias_mix,
    bias_group,
    step_bias,
    decay_log,
    skip_gain,
    gate_gain,
    out_weight,
    norm_second,
    up_weight,
    down_weight,
):
    rows_dev, heads_dev, head_dim, state_size = ssm_state.shape
    mix_dev = mix_weight.shape[2]
    group_dev = group_weight.shape[2]
    groups_dev = group_dev // state_size
    rows, width_dev = residual.shape
    n_req, n_head = lax.axis_size("req"), lax.axis_size("head")
    width_all = width_dev * n_req
    taps_all = conv_mix.shape[0]
    steps_pad = -heads_dev % 128
    sums = project(
        residual,
        norm_first,
        mix_weight.reshape(width_dev, 2 * mix_dev),
        group_weight.reshape(width_dev, 2 * group_dev),
        jnp.pad(step_weight, ((0, 0), (0, steps_pad))),
        n_req,
        n_head,
        width_all,
    )
    gate_z = sums[:, :mix_dev]
    mix_in = sums[:, mix_dev : 2 * mix_dev]
    group_in = sums[:, 2 * mix_dev : 2 * mix_dev + 2 * group_dev].reshape(rows_dev, 2, group_dev)
    step_raw = sums[:, 2 * mix_dev + 2 * group_dev : 2 * mix_dev + 2 * group_dev + heads_dev]
    valid = jnp.minimum(lengths, taps_all - 1)
    slots = jnp.arange(taps_all - 1)
    keep = (slots[None, :] >= (taps_all - 1 - valid)[:, None]).astype(F32)
    window_mix = jnp.concatenate([tail_mix * keep[:, :, None], mix_in[:, None, :]], axis=1)
    window_group = jnp.concatenate([tail_group * keep[:, :, None, None], group_in[:, None]], axis=1)
    conv_x = jax.nn.silu(jnp.sum(window_mix * conv_mix[None], axis=1) + bias_mix)
    conv_bc = jax.nn.silu(jnp.sum(window_group * conv_group[None], axis=1) + bias_group)
    step_size = jax.nn.softplus(step_raw + step_bias)
    alive = (lengths > 0).astype(F32)
    decay = jnp.exp(-step_size * jnp.exp(decay_log)) * alive[:, None]
    stride = jnp.repeat(step_size, head_dim, axis=1) * conv_x
    state_out, readout = state_step(decay, stride, conv_bc[:, 0], conv_bc[:, 1], ssm_state)
    mixed = readout + jnp.repeat(skip_gain, head_dim)[None, :] * conv_x
    gated = mixed * jax.nn.silu(gate_z)
    grouped = gated.reshape(rows_dev, groups_dev, -1)
    inverse = lax.rsqrt(jnp.mean(grouped * grouped, axis=2, keepdims=True) + eps)
    normed_y = ((grouped * inverse).reshape(rows_dev, mix_dev) * gate_gain).astype(BF16)
    residual_out = mlp(
        residual, normed_y, norm_second, out_weight, up_weight, down_weight, n_req, n_head, width_all
    )
    return (residual_out, state_out, window_mix[:, 1:], window_group[:, 1:])


def solution(mesh):
    return jax.shard_map(
        on_device,
        mesh=mesh,
        in_specs=(
            P(None, "req"),
            P("req"),
            P("req", "head", None, None),
            P("req", None, "head"),
            P("req", None, None, "head"),
            P("req"),
            P("req", None, "head"),
            P("req", None, "head"),
            P("req", "head"),
            P(None, "head"),
            P(None, None, "head"),
            P("head"),
            P(None, "head"),
            P("head"),
            P("head"),
            P("head"),
            P("head"),
            P("head", "req"),
            P("req"),
            P("req", "head"),
            P("head", "req"),
        ),
        out_specs=(
            P(None, "req"),
            P("req", "head", None, None),
            P("req", None, "head"),
            P("req", None, None, "head"),
        ),
        check_vma=False,
    )
```

```python
import functools

import jax
import jax.numpy as jnp
from jax import lax
from jax.experimental import pallas as pl
from jax.experimental.pallas import tpu as pltpu
from jax.sharding import PartitionSpec as P

eps = 1e-05
MESH = pl.DeviceIdType.MESH
F32 = jnp.float32
BF16 = jnp.bfloat16
VMEM = pltpu.VMEM


def spans(total, size):
    return [(s, min(size, total - s)) for s in range(0, total, size)]


def remote(src, dst, send, recv, target):
    return pltpu.make_async_remote_copy(
        src_ref=src,
        dst_ref=dst,
        send_sem=send,
        recv_sem=recv,
        device_id=target,
        device_id_type=MESH,
    )


class Place:
    def __init__(self, n_req, n_head):
        self.n_hi = n_req // 2
        self.n_head = n_head
        req = lax.axis_index("req")
        self.head = lax.axis_index("head")
        self.req = req
        self.hi = req // 2
        self.lo = lax.rem(req, 2)
        self.pair = (self.hi * 2 + 1 - self.lo, self.head)

    def hi_at(self, step):
        return lax.rem(self.hi + step + self.n_hi, self.n_hi)

    def column(self, step):
        return (self.hi_at(step) * 2 + self.lo, self.head)

    def head_at(self, step):
        return lax.rem(self.head + step + self.n_head, self.n_head)

    def heads(self, step):
        return (self.req, self.head_at(step))

    def greet(self, with_heads):
        barrier = pltpu.get_barrier_semaphore()
        peers = [self.pair] + [self.column(k) for k in range(1, self.n_hi)]
        if with_heads:
            peers += [self.heads(k) for k in range(1, self.n_head)]
        for peer in peers:
            pl.semaphore_signal(barrier, inc=1, device_id=peer, device_id_type=MESH)
        pl.semaphore_wait(barrier, len(peers))


class Scatter:
    def __init__(self, place, index, cols, part, first, mid, second, sems):
        self.place = place
        self.part, self.first, self.mid, self.second = part, first, mid, second
        self.cols = cols
        pair_send, pair_recv, col_send, col_recv = sems
        n_hi = place.n_hi
        self.to_pair = remote(
            part.at[:, 1 - place.lo, :, cols],
            first.at[:, :, cols],
            pair_send.at[index],
            pair_recv.at[index],
            place.pair,
        )
        self.to_col = [
            remote(
                mid.at[place.hi_at(k), :, cols],
                second.at[k - 1, :, cols],
                col_send.at[index, k - 1],
                col_recv.at[index, k - 1],
                place.column(k),
            )
            for k in range(1, n_hi)
        ]

    def send_pair(self):
        self.to_pair.start()

    def send_column(self):
        place, cols = self.place, self.cols
        self.to_pair.wait_recv()
        for k, copy in enumerate(self.to_col):
            there = place.hi_at(k + 1)
            both = self.part[there, place.lo, :, cols].astype(F32) + self.first[there, :, cols].astype(F32)
            self.mid[there, :, cols] = both.astype(self.mid.dtype)
            copy.start()

    def total(self):
        place, cols = self.place, self.cols
        here = place.hi
        value = self.part[here, place.lo, :, cols].astype(F32) + self.first[here, :, cols].astype(F32)
        for k, copy in enumerate(self.to_col):
            copy.wait_recv()
            value = value + self.second[k, :, cols].astype(F32)
        return value

    def finish(self):
        self.to_pair.wait_send()
        for copy in self.to_col:
            copy.wait_send()


class Gather:
    def __init__(self, place, index, cols, every, sems):
        self.place = place
        col_send, col_recv, pair_send, pair_recv = sems
        n_hi = place.n_hi
        mine = every.at[place.hi, place.lo, :, cols]
        self.to_col = [
            remote(mine, mine, col_send.at[index, k - 1], col_recv.at[index, k - 1], place.column(k))
            for k in range(1, n_hi)
        ]
        self.to_pair = []
        self.from_pair = []
        for k in range(n_hi):
            block = every.at[place.hi_at(-k), place.lo, :, cols]
            self.to_pair.append(remote(block, block, pair_send.at[index, k], pair_recv.at[index, k], place.pair))
            landed = every.at[place.hi_at(-k), 1 - place.lo, :, cols]
            self.from_pair.append(remote(landed, landed, pair_send.at[index, k], pair_recv.at[index, k], place.pair))
        self.from_col = []
        for k in range(1, n_hi):
            block = every.at[place.hi_at(-k), place.lo, :, cols]
            self.from_col.append(
                remote(block, block, col_send.at[index, k - 1], col_recv.at[index, k - 1], place.column(k))
            )

    def send(self):
        for copy in self.to_col:
            copy.start()
        self.to_pair[0].start()

    def forward(self):
        for k, copy in enumerate(self.from_col):
            copy.wait_recv()
            self.to_pair[k + 1].start()

    def land(self):
        for copy in self.from_pair:
            copy.wait_recv()

    def finish(self):
        for copy in self.to_col + self.to_pair:
            copy.wait_send()


def project_kernel(
    n_req, n_head, width_all, chunks, residual, gain, mix_w, group_w, step_w, out,
    part, first, mid, second, squares, first_sq, mid_sq, second_sq,
    pair_send, pair_recv, col_send, col_recv,
):
    place = Place(n_req, n_head)
    place.greet(False)
    sems = (pair_send, pair_recv, col_send, col_recv)
    n_hi = place.n_hi
    rows = residual.shape[0]
    rows_dev = rows // n_req
    wide = residual[...].astype(F32)
    sums = jnp.sum(wide * wide, axis=1, keepdims=True)
    squares[...] = jnp.broadcast_to(sums, (rows, 128)).reshape(n_hi, 2, rows_dev, 128)
    norm = Scatter(place, len(chunks), slice(None), squares, first_sq, mid_sq, second_sq, sems)
    norm.send_pair()
    scaled = (wide * gain[...]).astype(BF16)
    mix = mix_w.shape[1]
    heads = step_w.shape[0]
    steps = step_w[...]
    if heads % 128:
        steps = jnp.concatenate([steps, jnp.zeros((-heads % 128, steps.shape[1]), BF16)], axis=0)
    moves = []
    for c, (s, w) in enumerate(chunks):
        if s < mix:
            product = jnp.dot(scaled, mix_w[:, s : s + w], preferred_element_type=F32)
        else:
            product = jnp.concatenate(
                [
                    jnp.dot(scaled, group_w[...], preferred_element_type=F32),
                    lax.dot_general(scaled, steps, (((1,), (1,)), ((), ())), preferred_element_type=F32),
                ],
                axis=1,
            )
        part[:, :, :, s : s + w] = product.astype(BF16).reshape(n_hi, 2, rows_dev, w)
        moves.append(Scatter(place, c, pl.ds(s, w), part, first, mid, second, sems))
        moves[-1].send_pair()
    norm.send_column()
    inverse = None
    for c in range(len(moves) + 1):
        if c < len(moves):
            moves[c].send_column()
        if c == 0:
            inverse = lax.rsqrt(norm.total()[:, :1] / width_all + eps)
        else:
            s, w = chunks[c - 1]
            out[:, s : s + w] = moves[c - 1].total() * inverse
    norm.finish()
    for move in moves:
        move.finish()


def project(residual, gain, mix_w, group_w, step_w, n_req, n_head, width_all):
    rows, width = residual.shape
    mix, rest = mix_w.shape[1], group_w.shape[1] + -(-step_w.shape[0] // 128) * 128
    n = mix + rest
    rows_dev = rows // n_req
    n_hi = n_req // 2
    chunks = spans(mix, 512) + [(mix, rest)]
    count = len(chunks) + 1
    dma = pltpu.SemaphoreType.DMA
    vmem = pl.BlockSpec(memory_space=VMEM)
    return pl.pallas_call(
        functools.partial(project_kernel, n_req, n_head, width_all, chunks),
        out_shape=jax.ShapeDtypeStruct((rows_dev, n), F32),
        in_specs=[vmem] * 5,
        out_specs=vmem,
        scratch_shapes=[
            VMEM((n_hi, 2, rows_dev, n), BF16),
            VMEM((n_hi, rows_dev, n), BF16),
            VMEM((n_hi, rows_dev, n), BF16),
            VMEM((n_hi - 1, rows_dev, n), BF16),
            VMEM((n_hi, 2, rows_dev, 128), F32),
            VMEM((n_hi, rows_dev, 128), F32),
            VMEM((n_hi, rows_dev, 128), F32),
            VMEM((n_hi - 1, rows_dev, 128), F32),
            dma((count,)),
            dma((count,)),
            dma((count, n_hi - 1)),
            dma((count, n_hi - 1)),
        ],
        compiler_params=pltpu.CompilerParams(
            collective_id=0, has_side_effects=True, vmem_limit_bytes=32 * 1024 * 1024
        ),
    )(residual, gain.reshape(1, width), mix_w, group_w, step_w)


def state_kernel(batch, groups, per_group, head_dim, lengths, decay, stride_t, b_all, c_all, prior, updated, readout, left):
    turn = pl.program_id(0)
    rows, state = b_all.shape[0], prior.shape[3]

    @pl.when(turn == 0)
    def _():
        wide = stride_t[...]
        high = wide.astype(BF16)
        low = (wide - high.astype(F32)).astype(BF16)
        lane = lax.broadcasted_iota(jnp.int32, wide.shape, 1)
        left[...] = jnp.where(lane < 2 * rows, high.astype(F32), low.astype(F32)).astype(BF16)

    line = lax.broadcasted_iota(jnp.int32, (3 * rows, state), 0)
    middle = (line >= rows) & (line < 2 * rows)
    span = per_group * head_dim
    for i in range(batch):
        row = turn * batch + i
        chosen = lax.rem(line, rows) == row
        alive = jnp.where(lengths[row] > 0, 1.0, 0.0)
        own_row = lax.broadcasted_iota(jnp.int32, (rows, state), 0) == row
        for g in range(groups):
            b = b_all[:, g * state : (g + 1) * state]
            b = jnp.concatenate([b, b, b], axis=0)
            b_high = b.astype(BF16).astype(F32)
            b = jnp.where(chosen, jnp.where(middle, b - b_high, b_high), 0.0).astype(BF16)
            c = c_all[:, g * state : (g + 1) * state]
            c = jnp.sum(jnp.where(own_row, c, 0.0), axis=0, keepdims=True)
            c_high = c.astype(BF16).astype(F32)
            place = lax.broadcasted_iota(jnp.int32, (16, state), 0)
            c = jnp.where(place == 0, c_high, jnp.where(place == 1, c - c_high, 0.0)).astype(BF16)
            outer = jnp.dot(left[g * span : (g + 1) * span, :], b, preferred_element_type=F32)
            pieces = []
            for e in range(per_group):
                h = g * per_group + e
                value = (decay[row, h] * alive) * prior[i, h] + outer[e * head_dim : (e + 1) * head_dim]
                updated[i, h] = value
                pieces.append(value.astype(BF16))
            block = jnp.concatenate(pieces, axis=0)
            found = lax.dot_general(c, block, (((1,), (1,)), ((), ())), preferred_element_type=F32)
            readout[i, :, g * span : (g + 1) * span] = jnp.sum(found, axis=0, keepdims=True)


def state_step(lengths, decay, stride, b_vector, c_vector, prior):
    rows, heads, head_dim, state = prior.shape
    groups = b_vector.shape[1] // state
    turned = stride.T
    vmem = pl.BlockSpec(memory_space=VMEM)
    batch = 2 if rows % 2 == 0 else 1
    block = pl.BlockSpec((batch, heads, head_dim, state), lambda r: (r, 0, 0, 0))
    mix = heads * head_dim
    updated, readout = pl.pallas_call(
        functools.partial(state_kernel, batch, groups, heads // groups, head_dim),
        grid=(rows // batch,),
        out_shape=(
            jax.ShapeDtypeStruct(prior.shape, F32),
            jax.ShapeDtypeStruct((rows, 1, mix), F32),
        ),
        in_specs=[pl.BlockSpec(memory_space=pltpu.SMEM)] * 2 + [vmem, vmem, vmem, block],
        out_specs=(block, pl.BlockSpec((batch, 1, mix), lambda r: (r, 0, 0))),
        scratch_shapes=[VMEM((mix, 3 * rows), BF16)],
        compiler_params=pltpu.CompilerParams(vmem_limit_bytes=48 * 1024 * 1024),
        cost_estimate=pl.CostEstimate(flops=4 * prior.size * 48, bytes_accessed=8 * prior.size, transcendentals=0),
    )(lengths, decay, jnp.concatenate([turned, turned, turned], axis=1), b_vector, c_vector, prior)
    return updated, readout.reshape(rows, mix)


def mlp_kernel(
    n_req, n_head, width_all, y_chunks, chunks,
    residual, y_own, gain, out_w, up_w, down_w, out,
    out_v, up_v, down_v, y_all, partial, partial_in, mid_all, act, first, mid, second,
    squares, first_sq, mid_sq, second_sq, hidden, result,
    load, y_cs, y_cr, y_ps, y_pr, h_send, h_recv, g_send, g_recv,
    s_ps, s_pr, s_cs, s_cr, a_cs, a_cr, a_ps, a_pr, h2_send, h2_recv, g2_send, g2_recv,
):
    loads = [
        pltpu.make_async_copy(src, dst, load.at[i])
        for i, (src, dst) in enumerate([(out_w, out_v), (up_w, up_v), (down_w, down_v)])
    ]
    for copy in loads:
        copy.start()
    place = Place(n_req, n_head)
    place.greet(True)
    n_hi = place.n_hi
    rows = residual.shape[0]
    width = residual.shape[1]
    rows_dev = rows // n_req
    rows_head = rows // n_head
    at_head = pl.multiple_of(place.head * rows_head, rows_head)

    def spread(send_from, land_in, send, recv):
        copies = []
        for k in range(1, n_head):
            copies.append(
                remote(
                    send_from(place.head_at(k)), land_in(k), send.at[k - 1], recv.at[k - 1], place.heads(k)
                )
            )
            copies[-1].start()
        return copies

    def block_of(ref, index):
        return ref.at[pl.ds(pl.multiple_of(index * rows_head, rows_head), rows_head)]

    def head_sum(send, recv, landing):
        copies = spread(lambda h: block_of(partial, h), lambda k: landing.at[k - 1], send, recv)
        total = partial[pl.ds(at_head, rows_head), :].astype(F32)
        for k, copy in enumerate(copies):
            copy.wait_recv()
            total = total + landing[k].astype(F32)
        return total, copies

    def head_gather(ref, send, recv):
        mine = block_of(ref, place.head)
        copies = spread(lambda h: mine, lambda k: mine, send, recv)
        for k in range(1, n_head):
            there = block_of(ref, place.head_at(-k))
            remote(there, there, send.at[k - 1], recv.at[k - 1], place.heads(k)).wait_recv()
        return copies

    pending = []
    y_all[place.hi, place.lo] = y_own[...]
    gathers = [
        Gather(place, c, pl.ds(s, w), y_all, (y_cs, y_cr, y_ps, y_pr)) for c, (s, w) in enumerate(y_chunks)
    ]
    for move in gathers:
        move.send()
    for move in gathers:
        move.forward()
    loads[0].wait()
    mixer = None
    for move, (s, w) in zip(gathers, y_chunks):
        move.land()
        term = jnp.dot(
            y_all[:, :, :, s : s + w].reshape(rows, w), out_v[s : s + w, :], preferred_element_type=F32
        )
        mixer = term if mixer is None else mixer + term
    partial[...] = mixer.astype(BF16)
    total, copies = head_sum(h_send, h_recv, partial_in.at[0])
    pending += gathers
    for copy in copies:
        copy.wait_send()
    mid_all[pl.ds(at_head, rows_head), :] = (
        residual[pl.ds(at_head, rows_head), :].astype(F32) + total
    ).astype(BF16)
    copies = head_gather(mid_all, g_send, g_recv)
    for copy in copies:
        copy.wait_send()

    wide = mid_all[...].astype(F32)
    sums = jnp.sum(wide * wide, axis=1, keepdims=True)
    squares[...] = jnp.broadcast_to(sums, (rows, 128)).reshape(n_hi, 2, rows_dev, 128)
    sems = (s_ps, s_pr, s_cs, s_cr)
    norm = Scatter(place, len(chunks), slice(None), squares, first_sq, mid_sq, second_sq, sems)
    norm.send_pair()
    scaled = (wide * gain[...]).astype(BF16)
    moves = []
    shares = []
    loads[1].wait()
    for c, (s, w) in enumerate(chunks):
        piece = jnp.dot(scaled, up_v[:, s : s + w], preferred_element_type=F32).astype(BF16)
        act[:, :, :, s : s + w] = piece.reshape(n_hi, 2, rows_dev, w)
        moves.append(Scatter(place, c, pl.ds(s, w), act, first, mid, second, sems))
        moves[-1].send_pair()
        shares.append(Gather(place, c, pl.ds(s, w), hidden, (a_cs, a_cr, a_ps, a_pr)))
    norm.send_column()
    loads[2].wait()
    count = len(chunks)
    inverse = None
    projected = None
    for step in range(count + 3):
        if step < count:
            moves[step].send_column()
        c = step - 1
        if 0 <= c < count:
            if inverse is None:
                inverse = lax.rsqrt(norm.total()[:, :1] / width_all + eps)
            s, w = chunks[c]
            share = jnp.maximum(moves[c].total() * inverse, 0.0)
            hidden[place.hi, place.lo, :, pl.ds(s, w)] = (share * share).astype(BF16)
            shares[c].send()
        c = step - 2
        if 0 <= c < count:
            shares[c].forward()
        c = step - 3
        if 0 <= c < count:
            shares[c].land()
            s, w = chunks[c]
            term = jnp.dot(
                hidden[:, :, :, s : s + w].reshape(rows, w), down_v[s : s + w, :], preferred_element_type=F32
            )
            projected = term if projected is None else projected + term
    partial[...] = projected.astype(BF16)
    total, copies = head_sum(h2_send, h2_recv, partial_in.at[1])
    for copy in copies:
        copy.wait_send()
    result[pl.ds(at_head, rows_head), :] = (
        mid_all[pl.ds(at_head, rows_head), :].astype(F32) + total
    ).astype(BF16)
    copies = head_gather(result, g2_send, g2_recv)
    out[...] = result[...]
    for copy in copies:
        copy.wait_send()
    norm.finish()
    for move in pending + moves + shares:
        move.finish()


def mlp(residual, y_own, gain, out_w, up_w, down_w, n_req, n_head, width_all):
    rows, width = residual.shape
    rows_dev, mix = y_own.shape
    ff = up_w.shape[1]
    n_hi = n_req // 2
    y_chunks = spans(mix, 512)
    chunks = spans(ff, 512)
    count, y_count = len(chunks), len(y_chunks)
    rows_head = rows // n_head
    dma = pltpu.SemaphoreType.DMA
    vmem = pl.BlockSpec(memory_space=VMEM)
    anywhere = pl.BlockSpec(memory_space=pl.ANY)
    n_col, n_side = n_hi - 1, n_head - 1
    return pl.pallas_call(
        functools.partial(mlp_kernel, n_req, n_head, width_all, y_chunks, chunks),
        out_shape=jax.ShapeDtypeStruct((rows, width), BF16),
        in_specs=[vmem, vmem, vmem, anywhere, anywhere, anywhere],
        out_specs=vmem,
        scratch_shapes=[
            VMEM(out_w.shape, BF16),
            VMEM(up_w.shape, BF16),
            VMEM(down_w.shape, BF16),
            VMEM((n_hi, 2, rows_dev, mix), BF16),
            VMEM((rows, width), BF16),
            VMEM((2, n_side, rows_head, width), BF16),
            VMEM((rows, width), BF16),
            VMEM((n_hi, 2, rows_dev, ff), BF16),
            VMEM((n_hi, rows_dev, ff), BF16),
            VMEM((n_hi, rows_dev, ff), BF16),
            VMEM((n_col, rows_dev, ff), BF16),
            VMEM((n_hi, 2, rows_dev, 128), F32),
            VMEM((n_hi, rows_dev, 128), F32),
            VMEM((n_hi, rows_dev, 128), F32),
            VMEM((n_col, rows_dev, 128), F32),
            VMEM((n_hi, 2, rows_dev, ff), BF16),
            VMEM((rows, width), BF16),
            dma((3,)),
            dma((y_count, n_col)),
            dma((y_count, n_col)),
            dma((y_count, n_hi)),
            dma((y_count, n_hi)),
            dma((n_side,)),
            dma((n_side,)),
            dma((n_side,)),
            dma((n_side,)),
            dma((count + 1,)),
            dma((count + 1,)),
            dma((count + 1, n_col)),
            dma((count + 1, n_col)),
            dma((count, n_col)),
            dma((count, n_col)),
            dma((count, n_hi)),
            dma((count, n_hi)),
            dma((n_side,)),
            dma((n_side,)),
            dma((n_side,)),
            dma((n_side,)),
        ],
        compiler_params=pltpu.CompilerParams(
            collective_id=1, has_side_effects=True, vmem_limit_bytes=52 * 1024 * 1024
        ),
    )(residual, y_own, gain.reshape(1, width), out_w, up_w, down_w)


def on_device(
    residual,
    lengths,
    ssm_state,
    tail_mix,
    tail_group,
    norm_first,
    mix_weight,
    group_weight,
    step_weight,
    conv_mix,
    conv_group,
    bias_mix,
    bias_group,
    step_bias,
    decay_log,
    skip_gain,
    gate_gain,
    out_weight,
    norm_second,
    up_weight,
    down_weight,
):
    rows_dev, heads_dev, head_dim, state_size = ssm_state.shape
    mix_dev = mix_weight.shape[2]
    group_dev = group_weight.shape[2]
    groups_dev = group_dev // state_size
    rows, width_dev = residual.shape
    n_req, n_head = lax.axis_size("req"), lax.axis_size("head")
    width_all = width_dev * n_req
    taps_all = conv_mix.shape[0]
    sums = project(
        residual,
        norm_first,
        mix_weight.reshape(width_dev, 2 * mix_dev),
        group_weight.reshape(width_dev, 2 * group_dev),
        step_weight.T,
        n_req,
        n_head,
        width_all,
    )
    gate_z = sums[:, :mix_dev]
    mix_in = sums[:, mix_dev : 2 * mix_dev]
    group_in = sums[:, 2 * mix_dev : 2 * mix_dev + 2 * group_dev].reshape(rows_dev, 2, group_dev)
    step_raw = sums[:, 2 * mix_dev + 2 * group_dev : 2 * mix_dev + 2 * group_dev + heads_dev]
    slots = jnp.arange(taps_all - 1)
    keep = (slots[None, :] + lengths[:, None] >= taps_all - 1).astype(F32)
    window_mix = jnp.concatenate([tail_mix * keep[:, :, None], mix_in[:, None, :]], axis=1)
    window_group = jnp.concatenate([tail_group * keep[:, :, None, None], group_in[:, None]], axis=1)
    conv_x = jax.nn.silu(jnp.sum(window_mix * conv_mix[None], axis=1) + bias_mix)
    conv_bc = jax.nn.silu(jnp.sum(window_group * conv_group[None], axis=1) + bias_group)
    step_size = jax.nn.softplus(step_raw + step_bias)
    decay = jnp.exp(-step_size * jnp.exp(decay_log))
    gains = jnp.broadcast_to(skip_gain[None, :], step_size.shape)
    repeated = jnp.repeat(jnp.concatenate([step_size, gains], axis=0), head_dim, axis=1)
    stride = repeated[:rows_dev] * conv_x
    state_out, readout = state_step(lengths, decay, stride, conv_bc[:, 0], conv_bc[:, 1], ssm_state)
    mixed = readout + repeated[rows_dev:] * conv_x
    gated = mixed * jax.nn.silu(gate_z)
    grouped = gated.reshape(rows_dev, groups_dev, -1)
    inverse = lax.rsqrt(jnp.mean(grouped * grouped, axis=2, keepdims=True) + eps)
    normed_y = ((grouped * inverse).reshape(rows_dev, mix_dev) * gate_gain).astype(BF16)
    residual_out = mlp(
        residual, normed_y, norm_second, out_weight, up_weight, down_weight, n_req, n_head, width_all
    )
    return (residual_out, state_out, window_mix[:, 1:], window_group[:, 1:])


def solution(mesh):
    return jax.shard_map(
        on_device,
        mesh=mesh,
        in_specs=(
            P(None, "req"),
            P("req"),
            P("req", "head", None, None),
            P("req", None, "head"),
            P("req", None, None, "head"),
            P("req"),
            P("req", None, "head"),
            P("req", None, "head"),
            P("req", "head"),
            P(None, "head"),
            P(None, None, "head"),
            P("head"),
            P(None, "head"),
            P("head"),
            P("head"),
            P("head"),
            P("head"),
            P("head", "req"),
            P("req"),
            P("req", "head"),
            P("head", "req"),
        ),
        out_specs=(
            P(None, "req"),
            P("req", "head", None, None),
            P("req", None, "head"),
            P("req", None, None, "head"),
        ),
        check_vma=False,
    )
```
